32 devices in a mesh: parts: 2 (over y), people: 4 (over z), markers: 4 (over x, core).
Axes of the slice: x: 2, y: 2, z: 4, core: 2. Of those that a mesh axis runs over, the one named last changes fastest.
Arguments:
- dosages: float32 [4096, 8192], P(('parts', 'people'), 'markers'), parts along dimension 0, may hold values from 0 to 2
- freq: float32 [16384], P(('parts', 'markers')), parts along dimension 0, may hold values from 0.05 to 0.5
- pair_cols: int32 [8, 4], P(('parts', 'people')), parts along dimension 0, may hold values from 0 to 3, as said below
- pair_count: int32 [8], P(('parts', 'people')), parts along dimension 0, may hold values from 1 to 4, as said below
Outputs:
- tiles: float32 [512, 32, 512], P('markers', ('parts', 'people')), parts along dimension 1
The draws below stay inside these ranges and needn't reach their ends.
There are 2 independent parts, one for each index of `parts`. The reference program is written for one: setup_inputs(seed, part) draws one part's arguments, and reference() takes and returns one part's arrays. A program takes and returns all parts, laid end to end along the dimension named above; each array names one. Nothing has to cross between parts.
Inputs may be any that keep to these rules, and one draw needn't show every extreme that they name: `pair_cols`: entry 0 of row r is r itself; every entry of row r is (r + k) mod 4 for some k from 0 to 7. Some row block r lists (r + min(s, 7)) mod 4 in slot s for every s, with all 4 tiles live. `pair_count`: some row block has all 4 listed tiles live.
All inputs are finite; a program needn't handle non-finite values.
Results may differ from the reference program's by a relative error of at most 0.0003.
Values may be sent and summed in bfloat16 or wider, within the bound.
A program may use at most 128 MiB of HBM per device.

```python
import math
import jax
import jax.numpy as jnp
from jax import lax

TILE = 512
MARKERS = 8192
SLOTS = 4
REACH = 7
BLOCKS = 4
PEOPLE = 2048
N_MARKERS = 4


def busiest_block(key):
    return jax.random.randint(jax.random.fold_in(key, 5), (), 0, BLOCKS)


def draw_pair_cols(key, part):
    chosen = busiest_block(key)
    key = jax.random.fold_in(key, 11)
    offsets = jax.random.randint(key, (BLOCKS, SLOTS), 1, REACH + 1)
    offsets = offsets.at[:, 0].set(0)
    offsets = offsets.at[chosen].set(jnp.minimum(jnp.arange(SLOTS, dtype=jnp.int32), REACH))
    row_ids = jnp.arange(BLOCKS, dtype=jnp.int32)[:, None]
    return ((row_ids + offsets) % BLOCKS).astype(jnp.int32)


def draw_pair_count(key, part):
    chosen = busiest_block(key)
    key = jax.random.fold_in(key, 23)
    counts = jax.random.randint(key, (BLOCKS,), 1, SLOTS + 1)
    return counts.at[chosen].set(SLOTS).astype(jnp.int32)


def level_of(stream_key, dims, pieces, smallest, top_value):
    def one(axis_at, parts):
        heights = jax.random.uniform(jax.random.fold_in(jax.random.fold_in(stream_key, 6), axis_at), (parts,), jnp.float32, smallest / len(pieces), top_value / len(pieces))
        return jnp.repeat(jnp.exp(heights), dims[axis_at] // parts).reshape((-1,) + (1,) * (len(dims) - axis_at - 1))

    loudness = one(*pieces[0])
    for cut in pieces[1:]:
        loudness = loudness * one(*cut)
    return loudness


def setup_inputs(seed: int = 0, part: int = 0) -> dict:
    seeds = jax.random.split(jax.random.key(seed), 5)
    part_splits = jax.random.split(jax.random.fold_in(seeds[4], part), 5)
    return {
        "dosages": jnp.clip(2.0 * jax.random.uniform(part_splits[0], (PEOPLE, MARKERS), jnp.float32) ** level_of(part_splits[0], (PEOPLE, MARKERS), ((0, 4), (1, 4)), -0.2, 0.2), 0.0, 2.0),
        "freq": jnp.clip(jnp.exp(math.log(0.5) - 2.3025851 * jax.random.uniform(part_splits[1], (MARKERS,), jnp.float32) ** level_of(part_splits[1], (MARKERS,), ((0, 4),), -0.2, 0.2)), 0.05, 0.5),
        "pair_cols": draw_pair_cols(jax.random.fold_in(jax.random.fold_in(seeds[4], part), 71), part),
        "pair_count": draw_pair_count(jax.random.fold_in(jax.random.fold_in(seeds[4], part), 71), part),
    }


def standardize(dosages, freq):
    doubled_freq = 2.0 * freq
    spread = jnp.sqrt(doubled_freq * (1.0 - freq))
    return ((dosages.astype(jnp.float32) - doubled_freq) / spread).astype(jnp.bfloat16)

def reference(dosages, freq, pair_cols, pair_count):
    standard = standardize(dosages, freq)
    grouped = standard.reshape(BLOCKS, TILE, N_MARKERS, MARKERS // N_MARKERS)

    def one_block(row_index):
        row_block = grouped[row_index].astype(jnp.float32)
        columns = jnp.take(grouped, pair_cols[row_index], axis=0).astype(jnp.float32)
        group_sums = jnp.einsum('igm,sjgm->gisj', row_block, columns) / MARKERS
        summed = lax.optimization_barrier(jnp.sum(group_sums, axis=0))
        live_mask = (jnp.arange(SLOTS, dtype=jnp.int32) < pair_count[row_index]).astype(jnp.float32)
        return summed * live_mask[None, :, None]
    all_blocks = lax.map(one_block, jnp.arange(BLOCKS, dtype=jnp.int32))
    return jnp.transpose(all_blocks, (1, 0, 2, 3)).reshape(TILE, BLOCKS * SLOTS, TILE)
```

```python
import functools

import jax
import jax.numpy as jnp
from jax import lax
from jax.experimental import pallas as pl
from jax.experimental.pallas import tpu as pltpu
from jax.sharding import PartitionSpec as P

MESH = pl.DeviceIdType.MESH
PIECES = 4


def standardize(dosages, freq):
    doubled_freq = 2.0 * freq
    spread = jnp.sqrt(doubled_freq * (1.0 - freq))
    return ((dosages - doubled_freq) / spread).astype(jnp.bfloat16)


def gather_all(markers, dosages, freq, pair_cols, pair_count):
    standard = standardize(dosages, freq)
    listed_cols = pair_cols[0]
    gathered = lax.all_gather(standard, "people", axis=0, tiled=True)
    sources = gathered.reshape(-1, standard.shape[0], standard.shape[1])
    slot_total = listed_cols.shape[0]
    live_count = pair_count[0]
    columns = jnp.take(sources, listed_cols, axis=0)
    partial_value = (
        jnp.einsum("im,sjm->isj", standard, columns, preferred_element_type=jnp.float32) / markers
    )
    live_mask = (jnp.arange(slot_total, dtype=jnp.int32) < live_count).astype(jnp.float32)
    partial_value = partial_value * live_mask[None, :, None]
    return lax.psum_scatter(partial_value, "markers", scatter_dimension=0, tiled=True)


OWN, OUT, OPP, FAR = range(4)


def make_jobs(tile):
    half, piece = tile // 2, tile // PIECES
    early = [(0, OWN, 0, tile), (0, OPP, 0, half), (0, OPP, half, half)]
    middle = [(1, OWN, 0, tile), (1, OUT, 0, tile), (0, OUT, 0, tile), (1, OPP, 0, tile)]
    late = [(b, FAR, k * piece, piece) for k in range(PIECES) for b in (1, 0)]
    return early, middle, late


def kernel(scale, dos_ref, freq_ref, out_ref, std, got, acc, crecv, xrecv, fin, ores,
           out_send, out_recv, opp_send, opp_recv, far_send, far_recv,
           c_send, c_recv, x_send, x_recv, r_send, r_recv):
    tile = std.shape[0]
    piece = tile // PIECES
    z = lax.axis_index("people")
    m = lax.axis_index("markers")
    x, c = m // 2, m % 2
    is_inner = jnp.logical_and(z >= 1, z <= 2)
    mate = z + 1 - 2 * (z % 2)
    opposite = 3 - z
    core_mate = 2 * x + 1 - c
    x_mate = 2 * (1 - x) + c

    barrier = pltpu.get_barrier_semaphore()

    def greet(**where):
        pl.semaphore_signal(barrier, inc=1, device_id=where, device_id_type=MESH)

    greet(people=mate)

    @pl.when(is_inner)
    def _():
        greet(people=opposite)
        greet(markers=core_mate)
        greet(markers=x_mate)

    def rows(k):
        return pl.ds(k * piece, piece)

    doubled = 2.0 * freq_ref[...]
    inverse = 1.0 / jnp.sqrt(doubled * (1.0 - freq_ref[...]))

    def fill(k):
        step = 16

        @pl.loop(0, piece // step)
        def _(t):
            at = pl.ds(pl.multiple_of(k * piece + t * step, step), step)
            std[at, :] = ((dos_ref[at, :] - doubled) * inverse).astype(jnp.bfloat16)

    def remote(src, dst, send, recv, **where):
        return pltpu.make_async_remote_copy(
            src_ref=src, dst_ref=dst, send_sem=send, recv_sem=recv,
            device_id=where, device_id_type=MESH)

    early, middle, late = make_jobs(tile)
    jobs = early + middle + late
    outward = [j for j, job in enumerate(jobs) if job[0] == 1]

    def to_mate(k):
        return remote(std.at[rows(k)], got.at[0, rows(k)], out_send.at[k], out_recv.at[k], people=mate)

    def to_opposite(k):
        return remote(std.at[rows(k)], got.at[1, rows(k)], opp_send.at[k], opp_recv.at[k], people=opposite)

    def forward(k):
        return remote(got.at[0, rows(k)], got.at[2, rows(k)], far_send.at[k], far_recv.at[k], people=opposite)

    def core_copy(j):
        b, col, lo, n = jobs[j]
        return remote(acc.at[b, col, :, 1 - c, :, pl.ds(lo, n)], crecv.at[b, col, :, :, pl.ds(lo, n)],
                      c_send.at[j], c_recv.at[j], markers=core_mate)

    def x_copy(j):
        b, col, lo, n = jobs[j]
        return remote(acc.at[b, col, 1 - x, c, :, pl.ds(lo, n)], xrecv.at[b, col, :, pl.ds(lo, n)],
                      x_send.at[j], x_recv.at[j], markers=x_mate)

    def result_copy(j):
        b, col, lo, n = jobs[j]
        return remote(fin.at[col, :, pl.ds(lo, n)], ores.at[col, :, pl.ds(lo, n)],
                      r_send.at[j], r_recv.at[j], people=mate)

    @pl.when(jnp.logical_not(is_inner))
    def _():
        fill(0)
        pl.semaphore_wait(barrier, 1)
        to_mate(0).start()
        for k in range(1, PIECES):
            fill(k)
            to_mate(k).start()
        for k in range(PIECES):
            to_mate(k).wait_send()
        for j in outward:
            _, col, lo, n = jobs[j]
            result_copy(j).wait_recv()
            out_ref[col, :, pl.ds(lo, n)] = ores[col, :, pl.ds(lo, n)]

    @pl.when(is_inner)
    def _():
        fill(0)
        pl.semaphore_wait(barrier, 4)
        to_opposite(0).start()
        for k in range(1, PIECES):
            fill(k)
            to_opposite(k).start()

        def compute(j):
            b, col, lo, n = jobs[j]
            height = tile // 4

            @pl.loop(0, 2)
            def _(h):
                left_rows = pl.ds(pl.multiple_of(h * 2 * height, 2 * height), 2 * height)
                left = std[left_rows, :] if b == 0 else got[0, left_rows, :]
                right = std[pl.ds(lo, n), :] if col == OWN else got[col - 1, pl.ds(lo, n), :]
                product = lax.dot_general(left, right, (((1,), (1,)), ((), ())),
                                          preferred_element_type=jnp.float32)
                acc[b, col, h, 0, :, pl.ds(lo, n)] = product[:height]
                acc[b, col, h, 1, :, pl.ds(lo, n)] = product[height:]
            core_copy(j).start()

        def add_core(j):
            b, col, lo, n = jobs[j]
            core_copy(j).wait_recv()
            at = pl.ds(lo, n)
            acc[b, col, 1 - x, c, :, at] += crecv[b, col, 1 - x, :, at]
            x_copy(j).start()
            acc[b, col, x, c, :, at] += crecv[b, col, x, :, at]

        def finish(j):
            b, col, lo, n = jobs[j]
            at = pl.ds(lo, n)
            x_copy(j).wait_recv()
            value = (acc[b, col, x, c, :, at] + xrecv[b, col, :, at]) * scale
            if b == 1:
                fin[col, :, at] = value
                result_copy(j).start()
            else:
                out_ref[col, :, at] = value

        def arrive(k):
            to_mate(k).wait_recv()
            forward(k).start()

        done = {"x": 0, "f": 0}

        def push_x(upto):
            while done["x"] < upto:
                add_core(done["x"])
                done["x"] += 1

        def push_f(upto):
            while done["f"] < upto:
                finish(done["f"])
                done["f"] += 1

        compute(0)
        arrive(0)
        push_x(1)
        arrive(1)
        to_opposite(0).wait_recv()
        to_opposite(1).wait_recv()
        compute(1)
        arrive(2)
        push_x(2)
        push_f(1)
        to_opposite(2).wait_recv()
        to_opposite(3).wait_recv()
        compute(2)
        arrive(3)
        push_x(3)
        for j in range(3, 7):
            compute(j)
            push_x(j)
            push_f(j - 2)
        push_x(7)
        for k in range(PIECES):
            forward(k).wait_recv()
            j = 7 + 2 * k
            compute(j)
            compute(j + 1)
            push_x(j + 2)
            push_f(j)
        push_f(len(jobs))
        for k in range(PIECES):
            to_opposite(k).wait_send()
            forward(k).wait_send()
        for j in range(len(jobs)):
            core_copy(j).wait_send()
            x_copy(j).wait_send()
        for j in outward:
            result_copy(j).wait_send()


def four_blocks(markers, dosages, freq, pair_cols, pair_count):
    tile, depth = dosages.shape
    height = tile // 4
    early, middle, late = make_jobs(tile)
    n_jobs = len(early + middle + late)
    dma = pltpu.SemaphoreType.DMA
    vmem = pl.BlockSpec(memory_space=pltpu.VMEM)
    by_name = pl.pallas_call(
        functools.partial(kernel, 1.0 / markers),
        out_shape=jax.ShapeDtypeStruct((4, height, tile), jnp.float32),
        in_specs=[vmem, vmem],
        out_specs=vmem,
        scratch_shapes=[
            pltpu.VMEM((tile, depth), jnp.bfloat16),
            pltpu.VMEM((3, tile, depth), jnp.bfloat16),
            pltpu.VMEM((2, 4, 2, 2, height, tile), jnp.float32),
            pltpu.VMEM((2, 4, 2, height, tile), jnp.float32),
            pltpu.VMEM((2, 4, height, tile), jnp.float32),
            pltpu.VMEM((4, height, tile), jnp.float32),
            pltpu.VMEM((4, height, tile), jnp.float32),
        ] + [dma((PIECES,))] * 6 + [dma((n_jobs,))] * 6,
        compiler_params=pltpu.CompilerParams(
            collective_id=0, has_side_effects=True, vmem_limit_bytes=52 * 2**20),
        cost_estimate=pl.CostEstimate(
            flops=2 * 2 * tile * 4 * tile * depth, bytes_accessed=6 * tile * depth, transcendentals=0),
    )(dosages, freq.reshape(1, depth))

    low = lax.axis_index("people") < 2
    names = jnp.where(low, jnp.array([OUT, OWN, OPP, FAR], jnp.int32), jnp.array([FAR, OPP, OWN, OUT], jnp.int32))
    slots = pair_cols.shape[1]
    tiles = []
    for s in range(slots):
        name = jnp.sum(jnp.where(jnp.arange(4, dtype=jnp.int32) == pair_cols[0, s], names, 0))
        live = s < pair_count[0]
        value = jnp.zeros_like(by_name[0])
        for k in range(4):
            value = jnp.where(jnp.logical_and(live, name == k), by_name[k], value)
        tiles.append(value)
    return jnp.stack(tiles, axis=1)


def solution(mesh):
    in_specs = (
        P(("parts", "people"), "markers"),
        P(("parts", "markers")),
        P(("parts", "people"), None),
        P(("parts", "people")),
    )
    out_specs = P("markers", ("parts", "people"), None)

    def on_device(dosages, *rest):
        markers = dosages.shape[1] * mesh.shape["markers"]
        four = mesh.shape["people"] == 4 and mesh.shape["markers"] == 4
        return (four_blocks if four else gather_all)(markers, dosages, *rest)

    return jax.shard_map(
        on_device, mesh=mesh, in_specs=in_specs, out_specs=out_specs, check_vma=False
    )
```
